128 devices in a mesh: pipe: 8 (over z, core), tensor: 16 (over x, y).
Axes of the slice: x: 4, y: 4, z: 4, core: 2. Of those that a mesh axis runs over, the one named last changes fastest.
Arguments:
- tokens: bfloat16 [8, 128, 4096], P(None, 'tensor'), may hold values from -60 to 60
- norm_gain: float32 [8, 4096], P('pipe'), may hold values from 0.25 to 1.75
- gate_weight: bfloat16 [8, 4096, 14336], P('pipe', None, 'tensor'), may hold values from -0.09375 to 0.09375
- up_weight: bfloat16 [8, 4096, 14336], P('pipe', None, 'tensor'), may hold values from -0.09375 to 0.09375
- down_weight: bfloat16 [8, 14336, 4096], P('pipe', 'tensor'), may hold values from -0.046875 to 0.046875
Outputs:
- states: bfloat16 [8, 8, 128, 4096], P('pipe', None, 'tensor')
The draws below stay inside these ranges and needn't reach their ends.
All inputs are finite; a program needn't handle non-finite values.
Results may differ from the reference program's by a relative error of at most 0.019.
Values may be sent and summed in bfloat16 or wider, within the bound.
A program may use at most 128 MiB of HBM per device.

```python
import math
import jax
import jax.numpy as jnp
from jax import lax

D = 4096
FF = 14336
ROWS = 128
MB = 8
LAYERS = 8


def draw_tokens(key, part):
    key = jax.random.fold_in(key, 11)
    key_rows, key_cols, key_base = jax.random.split(key, 3)
    low = math.log(0.3)
    high = math.log(3.0)
    row_scale = jnp.exp(jax.random.uniform(key_rows, (MB, ROWS, 1), jnp.float32, low, high))
    col_scale = jnp.exp(jax.random.uniform(key_cols, (1, 1, D), jnp.float32, low, high))
    base = jnp.clip(jax.random.normal(key_base, (MB, ROWS, D), jnp.float32), -6.0, 6.0)
    return (base * row_scale * col_scale).astype(jnp.bfloat16)


def block_scale(rng, extent, pieces, low, top_value):
    loudness = 1.0
    for dim, parts in pieces:
        heights = jax.random.uniform(jax.random.fold_in(jax.random.fold_in(rng, 6), dim), (parts,), jnp.float32, low / len(pieces), top_value / len(pieces))
        loudness = loudness * jnp.repeat(jnp.exp(heights), extent[dim] // parts).reshape((-1,) + (1,) * (len(extent) - 1 - dim))
    return loudness


def normal_values(key, extent, width, bound, pieces=(), dtype=jnp.bfloat16):
    values = jax.random.normal(key, extent, jnp.float32) * width
    if len(pieces) > 0:
        values = block_scale(key, extent, pieces, -0.22, 0.18) * values
    return jnp.clip(values, min=-bound, max=bound).astype(dtype)


def setup_inputs(seed: int = 0) -> dict:
    keys = jax.random.split(jax.random.key(seed), 6)
    return {
        "tokens": draw_tokens(jax.random.fold_in(keys[5], 71), 0),
        "norm_gain": jnp.clip(1.0 + 0.15 * jax.random.normal(keys[1], (LAYERS, D), jnp.float32), 0.25, 1.75),
        "gate_weight": normal_values(keys[2], (LAYERS, D, FF), D ** -0.5, 0.09375, ((0, 8), (2, 16))),
        "up_weight": normal_values(keys[3], (LAYERS, D, FF), D ** -0.5, 0.09375, ((0, 8), (2, 16))),
        "down_weight": normal_values(keys[4], (LAYERS, FF, D), FF ** -0.5, 0.046875, ((0, 8), (1, 16))),
    }


def normalize(row_block, scale_gain):
    values = row_block.astype(jnp.float32)
    inv_rms = jax.lax.rsqrt(lax.optimization_barrier(jnp.mean(values * values, axis=-1, keepdims=True)) + 1e-05)
    return (values * inv_rms * scale_gain.astype(jnp.float32)).astype(jnp.bfloat16)

def reference(tokens, norm_gain, gate_weight, up_weight, down_weight):
    residual_rows = tokens.reshape(MB * ROWS, D)
    collected = []
    for layer_idx in range(LAYERS):
        normed = normalize(residual_rows, norm_gain[layer_idx])
        gate_out = jnp.dot(normed, gate_weight[layer_idx], preferred_element_type=jnp.float32)
        up_out = jnp.dot(normed, up_weight[layer_idx], preferred_element_type=jnp.float32)
        hidden = (jax.nn.silu(gate_out) * up_out).astype(jnp.bfloat16)
        branch = jnp.dot(hidden, down_weight[layer_idx], preferred_element_type=jnp.float32)
        residual_rows = (residual_rows.astype(jnp.float32) + branch).astype(jnp.bfloat16)
        collected.append(residual_rows.reshape(MB, ROWS, D))
    return jnp.stack(collected)
```

```python
import functools

import jax
import jax.numpy as jnp
from jax import lax
from jax.experimental import pallas as pl
from jax.experimental.pallas import tpu as pltpu
from jax.sharding import PartitionSpec as P

MESH = pl.DeviceIdType.MESH
F32 = jnp.float32
BF16 = jnp.bfloat16

SIDE = 4
OWN = 8
CHUNK = SIDE * OWN
PIECE = 512


def kernel(
    stages, blocks, tokens, gain, w_gate_hbm, w_up_hbm, w_down_hbm, states,
    w_gate, w_up, w_down, act_a, act_b, part_a, part_b, sum_a, sum_b, send_a, send_b,
    out_a, out_b, tok_a, tok_b, normed, hidden, fresh, load_sem, recv_sem, send1_sem, send_sem, tok_sem,
):
    stage = lax.axis_index("pipe")
    place = lax.axis_index("tensor")
    x, y = place // SIDE, lax.rem(place, SIDE)
    half = act_a.shape[-1]
    pieces = half // PIECE

    def on(stage_to, x_to, y_to):
        return (stage_to, x_to * SIDE + y_to)

    def turn(value, step):
        return lax.rem(value + step, SIDE)

    loads = [
        pltpu.make_async_copy(source, target, load_sem.at[i])
        for i, (source, target) in enumerate(((w_gate_hbm, w_gate), (w_up_hbm, w_up), (w_down_hbm, w_down)))
    ]
    for load in loads:
        load.start()

    barrier = pltpu.get_barrier_semaphore()
    after, before = lax.rem(stage + 1, stages), lax.rem(stage + stages - 1, stages)
    greeted = 0
    for other in (stage, after, before):
        for step in range(1, SIDE):
            for target in (on(other, turn(x, step), y), on(other, x, turn(y, step))):
                pl.semaphore_signal(barrier, inc=1, device_id=target, device_id_type=MESH)
                greeted += 1
    for other in (after, before):
        pl.semaphore_signal(barrier, inc=1, device_id=on(other, x, y), device_id_type=MESH)
        greeted += 1
    pl.semaphore_wait(barrier, greeted)

    def remote(source, target, sent, received, device):
        return pltpu.make_async_remote_copy(
            src_ref=source, dst_ref=target, send_sem=sent, recv_sem=received, device_id=device, device_id_type=MESH
        )

    def wait_bytes(ref, sem):
        pltpu.make_async_copy(ref, ref, sem).wait()

    def spread_a(i, stage_to):
        for step in range(SIDE):
            remote(out_a.at[i], act_a.at[i, x], send_sem.at[2, i], recv_sem.at[4, i], on(stage_to, turn(x, step), y)).start()

    def spread_b(i, stage_to):
        for step in range(SIDE):
            remote(out_b.at[i], act_b.at[i, y], send_sem.at[3, i], recv_sem.at[5, i], on(stage_to, x, turn(y, step))).start()

    def spread_sent(i):
        wait_bytes(act_a.at[i], send_sem.at[2, i])
        wait_bytes(act_b.at[i], send_sem.at[3, i])

    @pl.when(stage == 1)
    def _():
        for pair in range(blocks // 2):
            rows = jnp.concatenate([tokens[2 * pair].astype(F32), tokens[2 * pair + 1].astype(F32)], axis=0).astype(BF16)
            tok_a[pair, y] = rows[:, :half]
            tok_b[pair, x] = rows[:, half:]
            for step in range(1, SIDE):
                remote(tok_a.at[pair, y], tok_a.at[pair, y], tok_sem.at[0, pair], tok_sem.at[2, pair], on(stage, x, turn(y, step))).start()
                remote(tok_b.at[pair, x], tok_b.at[pair, x], tok_sem.at[1, pair], tok_sem.at[3, pair], on(stage, turn(x, step), y)).start()

        def bring(pair, carry):
            wait_bytes(tok_a.at[pair, pl.ds(0, SIDE - 1)], tok_sem.at[2, pair])
            wait_bytes(tok_b.at[pair, pl.ds(0, SIDE - 1)], tok_sem.at[3, pair])
            for odd in range(2):
                i = 2 * pair + odd
                for tok, out in ((tok_a, out_a), (tok_b, out_b)):
                    out[i] = jnp.concatenate(
                        [tok[pair, k].astype(F32)[odd * OWN : (odd + 1) * OWN] for k in range(SIDE)], axis=0
                    ).astype(BF16)
                spread_a(i, stage - 1)
                spread_b(i, stage - 1)
            return carry

        lax.fori_loop(0, blocks // 2, bring, 0)

        def brought(pair, carry):
            wait_bytes(tok_a.at[pair, pl.ds(0, SIDE - 1)], tok_sem.at[0, pair])
            wait_bytes(tok_b.at[pair, pl.ds(0, SIDE - 1)], tok_sem.at[1, pair])
            for odd in range(2):
                spread_sent(2 * pair + odd)
            return carry

        lax.fori_loop(0, blocks // 2, brought, 0)

    for load in loads:
        load.wait()

    def normalize(i):
        for x_of in range(SIDE):
            for pair in range(SIDE // 2):
                values_a = act_a[i, x_of, 2 * pair * OWN : 2 * (pair + 1) * OWN, :].astype(F32)
                low = x_of // 2 * 2 * OWN
                at = x_of % 2 * OWN
                values_b = jnp.concatenate(
                    [
                        act_b[i, 2 * pair + k, low : low + 2 * OWN, :].astype(F32)[at : at + OWN]
                        for k in range(2)
                    ],
                    axis=0,
                )
                total = jnp.sum(values_a * values_a, axis=-1, keepdims=True) + jnp.sum(values_b * values_b, axis=-1, keepdims=True)
                scale = lax.rsqrt(total * (1.0 / (2 * half)) + 1e-05)
                row = x_of * CHUNK + 2 * pair * OWN
                normed[row : row + 2 * OWN, :half] = (values_a * scale * gain[:, :half]).astype(BF16)
                normed[row : row + 2 * OWN, half:] = (values_b * scale * gain[:, half:]).astype(BF16)

    def compute(i):
        slot = lax.rem(i, 2)
        wait_bytes(act_a.at[i], recv_sem.at[4, i])
        wait_bytes(act_b.at[i], recv_sem.at[5, i])
        normalize(i)
        gate = jnp.dot(normed[...], w_gate[...], preferred_element_type=F32)
        up = jnp.dot(normed[...], w_up[...], preferred_element_type=F32)
        hidden[...] = (gate / (1.0 + jnp.exp(-gate)) * up).astype(BF16)

        @pl.when(i >= 2)
        def _():
            wait_bytes(send_a.at[slot, pl.ds(0, SIDE - 1)], send1_sem.at[0, slot])
            wait_bytes(send_b.at[slot, pl.ds(0, SIDE - 1)], send1_sem.at[1, slot])

        def down_a(piece, carry):
            at = pl.ds(pl.multiple_of(piece * PIECE, PIECE), PIECE)
            share = jnp.dot(hidden[...], w_down[:, at], preferred_element_type=F32)
            for k in range(SIDE):
                send_a[slot, k, :, at] = share[k * CHUNK : (k + 1) * CHUNK].astype(BF16)
            return carry

        lax.fori_loop(0, pieces, down_a, 0)
        for step in range(1, SIDE):
            to = turn(x, step)
            remote(send_a.at[slot, to], part_a.at[i, step - 1], send1_sem.at[0, slot], recv_sem.at[0, i], on(stage, to, y)).start()

        def down_b(piece, carry):
            at = pl.ds(pl.multiple_of(piece * PIECE, PIECE), PIECE)
            from_w = pl.ds(pl.multiple_of(piece * PIECE + half, PIECE), PIECE)
            share = jnp.dot(hidden[...], w_down[:, from_w], preferred_element_type=F32)
            for k in range(SIDE):
                rows = [share[m * CHUNK + k * OWN : m * CHUNK + (k + 1) * OWN] for m in range(SIDE)]
                send_b[slot, k, :, at] = jnp.concatenate(rows, axis=0).astype(BF16)
            return carry

        lax.fori_loop(0, pieces, down_b, 0)
        for step in range(1, SIDE):
            to = turn(y, step)
            remote(send_b.at[slot, to], part_b.at[i, step - 1], send1_sem.at[1, slot], recv_sem.at[1, i], on(stage, x, to)).start()

    def reduce_line(i):
        slot = lax.rem(i, 2)

        def add(send, mine, part, total, entry):
            def one(piece, carry):
                at = pl.ds(pl.multiple_of(piece * PIECE, PIECE), PIECE)
                value = send[slot, mine, :, at].astype(F32)
                for k in range(SIDE - 1):
                    value += part[i, k, :, at].astype(F32)
                total[i, entry, :, at] = value.astype(BF16)
                return carry

            lax.fori_loop(0, pieces, one, 0)

        wait_bytes(part_a.at[i], recv_sem.at[0, i])
        add(send_a, x, part_a, sum_a, y)
        for step in range(1, SIDE):
            remote(sum_a.at[i, y], sum_a.at[i, y], send_sem.at[0, i], recv_sem.at[2, i], on(stage, x, turn(y, step))).start()
        wait_bytes(part_b.at[i], recv_sem.at[1, i])
        add(send_b, y, part_b, sum_b, x)
        for step in range(1, SIDE):
            remote(sum_b.at[i, x], sum_b.at[i, x], send_sem.at[1, i], recv_sem.at[3, i], on(stage, turn(x, step), y)).start()

    def finish(i):
        def add(act, mine, total, out, own_at, column):
            def one(piece, carry):
                at = pl.ds(pl.multiple_of(piece * PIECE, PIECE), PIECE)
                branch = total[i, 0, :, at].astype(F32)
                for k in range(1, SIDE):
                    branch += total[i, k, :, at].astype(F32)
                value = act[i, mine, :, at].astype(F32) + branch
                out[i, :, at] = value.astype(BF16)
                fresh[:, at] = value
                return carry

            lax.fori_loop(0, pieces, one, 0)
            own = fresh[pl.ds(pl.multiple_of(own_at * OWN, OWN), OWN), :]
            states[i, :, column : column + half] = own.astype(BF16)

        wait_bytes(sum_a.at[i, pl.ds(0, SIDE - 1)], recv_sem.at[2, i])
        add(act_a, x, sum_a, out_a, y, 0)

        @pl.when(stage < stages - 1)
        def _():
            spread_a(i, stage + 1)

        wait_bytes(sum_b.at[i, pl.ds(0, SIDE - 1)], recv_sem.at[3, i])
        add(act_b, y, sum_b, out_b, x, half)

        @pl.when(stage < stages - 1)
        def _():
            spread_b(i, stage + 1)

    def advance(i, carry):
        compute(i)

        @pl.when(i > 0)
        def _():
            finish(i - 1)

        reduce_line(i)
        return carry

    lax.fori_loop(0, blocks, advance, 0)
    finish(blocks - 1)

    def drain(i, carry):
        wait_bytes(sum_a.at[i, pl.ds(0, SIDE - 1)], send_sem.at[0, i])
        wait_bytes(sum_b.at[i, pl.ds(0, SIDE - 1)], send_sem.at[1, i])

        @pl.when(stage < stages - 1)
        def _():
            spread_sent(i)

        return carry

    lax.fori_loop(0, blocks, drain, 0)
    for slot in range(2):
        wait_bytes(send_a.at[slot, pl.ds(0, SIDE - 1)], send1_sem.at[0, slot])
        wait_bytes(send_b.at[slot, pl.ds(0, SIDE - 1)], send1_sem.at[1, slot])


def solution(mesh):
    stages = mesh.shape["pipe"]

    def local(tokens, norm_gain, gate_weight, up_weight, down_weight):
        blocks, _, width = tokens.shape
        units = gate_weight.shape[2]
        half = width // 2
        vmem = pl.BlockSpec(memory_space=pltpu.VMEM)
        hbm = pl.BlockSpec(memory_space=pl.ANY)
        dma = pltpu.SemaphoreType.DMA
        states = pl.pallas_call(
            functools.partial(kernel, stages, blocks),
            out_shape=jax.ShapeDtypeStruct(tokens.shape, BF16),
            in_specs=[vmem, vmem, hbm, hbm, hbm],
            out_specs=vmem,
            scratch_shapes=[
                pltpu.VMEM((width, units), BF16),
                pltpu.VMEM((width, units), BF16),
                pltpu.VMEM((units, width), BF16),
                pltpu.VMEM((blocks, SIDE, CHUNK, half), BF16),
                pltpu.VMEM((blocks, SIDE, CHUNK, half), BF16),
                pltpu.VMEM((blocks, SIDE - 1, CHUNK, half), BF16),
                pltpu.VMEM((blocks, SIDE - 1, CHUNK, half), BF16),
                pltpu.VMEM((blocks, SIDE, CHUNK, half), BF16),
                pltpu.VMEM((blocks, SIDE, CHUNK, half), BF16),
                pltpu.VMEM((2, SIDE, CHUNK, half), BF16),
                pltpu.VMEM((2, SIDE, CHUNK, half), BF16),
                pltpu.VMEM((blocks, CHUNK, half), BF16),
                pltpu.VMEM((blocks, CHUNK, half), BF16),
                pltpu.VMEM((blocks // 2, SIDE, 2 * OWN, half), BF16),
                pltpu.VMEM((blocks // 2, SIDE, 2 * OWN, half), BF16),
                pltpu.VMEM((SIDE * CHUNK, width), BF16),
                pltpu.VMEM((SIDE * CHUNK, units), BF16),
                pltpu.VMEM((CHUNK, half), F32),
                dma((3,)),
                dma((6, blocks)),
                dma((2, 2)),
                dma((4, blocks)),
                dma((4, blocks // 2)),
            ],
            compiler_params=pltpu.CompilerParams(
                collective_id=0, has_side_effects=True, vmem_limit_bytes=62 * 2**20
            ),
            cost_estimate=pl.CostEstimate(
                flops=2 * 3 * blocks * SIDE * CHUNK * width * units,
                bytes_accessed=6 * width * units,
                transcendentals=blocks * SIDE * CHUNK * units,
            ),
        )(tokens, norm_gain, gate_weight[0], up_weight[0], down_weight[0])
        return states[None]

    in_specs = (
        P(None, "tensor", None),
        P("pipe", None),
        P("pipe", None, "tensor"),
        P("pipe", None, "tensor"),
        P("pipe", "tensor", None),
    )
    out_specs = P("pipe", None, "tensor", None)
    return jax.shard_map(local, mesh=mesh, in_specs=in_specs, out_specs=out_specs, check_vma=False)
```

```python
import functools

import jax
import jax.numpy as jnp
from jax import lax
from jax.experimental import pallas as pl
from jax.experimental.pallas import tpu as pltpu
from jax.sharding import PartitionSpec as P

MESH = pl.DeviceIdType.MESH
F32 = jnp.float32
BF16 = jnp.bfloat16

SIDE = 4
OWN = 8
CHUNK = SIDE // 2 * OWN
PIECE = 1024
ORDER = (("down", 0), ("finish", 1), ("up", -1), ("line", 0))


def kernel(
    stages, blocks, tokens, gain, w_gate_hbm, w_up_hbm, w_down_hbm, states,
    w_gate, w_up, w_down, act_a, act_b, part_a, part_b, sum_a, sum_b, send_a, send_b,
    out_a, out_b, tok_a, tok_b, gate_sum, up_sum, squares, hidden, fresh, load_sem, recv_sem, send1_sem, send_sem, tok_sem,
):
    stage = lax.axis_index("pipe")
    place = lax.axis_index("tensor")
    x, y = place // SIDE, lax.rem(place, SIDE)
    pieces = act_a.shape[1]
    half = pieces * PIECE
    pairs = blocks // 4

    def on(stage_to, x_to, y_to):
        return (stage_to, x_to * SIDE + y_to)

    def turn(value, step):
        return lax.rem(value + step, SIDE)

    loads = []
    for p in range(pieces):
        for k in range(2):
            for j, (source, target) in enumerate(((w_gate_hbm, w_gate), (w_up_hbm, w_up))):
                loads.append(
                    pltpu.make_async_copy(
                        source.at[pl.ds(k * half + p * PIECE, PIECE)],
                        target.at[p, pl.ds(k * PIECE, PIECE)],
                        load_sem.at[(p * 2 + k) * 2 + j],
                    )
                )
    loads.append(pltpu.make_async_copy(w_down_hbm, w_down, load_sem.at[4 * pieces]))
    for load in loads:
        load.start()

    barrier = pltpu.get_barrier_semaphore()
    after, before = lax.rem(stage + 1, stages), lax.rem(stage + stages - 1, stages)
    greeted = 0
    for other in (stage, after, before):
        for step in range(1, SIDE):
            for target in (on(other, turn(x, step), y), on(other, x, turn(y, step))):
                pl.semaphore_signal(barrier, inc=1, device_id=target, device_id_type=MESH)
                greeted += 1
    for other in (after, before):
        pl.semaphore_signal(barrier, inc=1, device_id=on(other, x, y), device_id_type=MESH)
        greeted += 1
    pl.semaphore_wait(barrier, greeted)

    def remote(source, target, sent, received, device):
        return pltpu.make_async_remote_copy(
            src_ref=source, dst_ref=target, send_sem=sent, recv_sem=received, device_id=device, device_id_type=MESH
        )

    def wait_bytes(ref, sem):
        pltpu.make_async_copy(ref, ref, sem).wait()

    def spread_a(i, p, stage_to):
        for step in range(SIDE):
            remote(out_a.at[i, p], act_a.at[i, p, x], send_sem.at[2, i], recv_sem.at[4, i, p], on(stage_to, turn(x, step), y)).start()

    def spread_b(i, p, stage_to):
        for step in range(SIDE):
            remote(out_b.at[i, p], act_b.at[i, p, y], send_sem.at[3, i], recv_sem.at[5, i, p], on(stage_to, x, turn(y, step))).start()

    def spread_sent(i):
        wait_bytes(act_a.at[i], send_sem.at[2, i])
        wait_bytes(act_b.at[i], send_sem.at[3, i])

    @pl.when(stage == 1)
    def _():
        for pair in range(pairs):
            rows = jnp.concatenate([tokens[2 * pair].astype(F32), tokens[2 * pair + 1].astype(F32)], axis=0).astype(BF16)
            tok_a[pair, y] = rows[:, :half]
            tok_b[pair, x] = rows[:, half:]
            for step in range(1, SIDE):
                remote(tok_a.at[pair, y], tok_a.at[pair, y], tok_sem.at[0, pair], tok_sem.at[2, pair], on(stage, x, turn(y, step))).start()
                remote(tok_b.at[pair, x], tok_b.at[pair, x], tok_sem.at[1, pair], tok_sem.at[3, pair], on(stage, turn(x, step), y)).start()

        def bring(pair, carry):
            wait_bytes(tok_a.at[pair, pl.ds(0, SIDE - 1)], tok_sem.at[2, pair])
            wait_bytes(tok_b.at[pair, pl.ds(0, SIDE - 1)], tok_sem.at[3, pair])
            for half_of_pair in range(2):
                for parity in range(2):
                    i = 4 * pair + 2 * half_of_pair + parity
                    for p in range(pieces):
                        at = slice(p * PIECE, (p + 1) * PIECE)
                        own = slice(half_of_pair * OWN, (half_of_pair + 1) * OWN)
                        for tok, out, mine in ((tok_a, out_a, x), (tok_b, out_b, y)):
                            first = lax.rem(mine + parity, 2)
                            out[i, p] = jnp.concatenate(
                                [tok[pair, first + 2 * k, :, at].astype(F32)[own] for k in range(SIDE // 2)], axis=0
                            ).astype(BF16)
                        spread_a(i, p, stage - 1)
                        spread_b(i, p, stage - 1)
            return carry

        lax.fori_loop(0, pairs, bring, 0)

        def brought(pair, carry):
            wait_bytes(tok_a.at[pair, pl.ds(0, SIDE - 1)], tok_sem.at[0, pair])
            wait_bytes(tok_b.at[pair, pl.ds(0, SIDE - 1)], tok_sem.at[1, pair])
            for k in range(4):
                spread_sent(4 * pair + k)
            return carry

        lax.fori_loop(0, pairs, brought, 0)

    for load in loads:
        load.wait()

    def up(i):
        rows = SIDE * CHUNK
        parity = lax.rem(i, 2)

        for p in range(pieces):
            wait_bytes(act_a.at[i, p], recv_sem.at[4, i, p])
            wait_bytes(act_b.at[i, p], recv_sem.at[5, i, p])
            values_a = act_a[i, p].astype(F32).reshape(rows, PIECE)
            even = [act_b[i, p, 2 * j + parity].astype(F32) for j in range(SIDE // 2)]
            odd = [act_b[i, p, 2 * j + 1 - parity].astype(F32) for j in range(SIDE // 2)]
            values_b = jnp.concatenate(
                [
                    (odd if m % 2 else even)[j][m // 2 * OWN : (m // 2 + 1) * OWN]
                    for m in range(SIDE)
                    for j in range(SIDE // 2)
                ],
                axis=0,
            )
            square = jnp.zeros((rows, 128), F32)
            for values in (values_a, values_b):
                for lane in range(0, PIECE, 128):
                    part = values[:, lane : lane + 128]
                    square += part * part
            scaled = jnp.concatenate(
                [
                    (values_a * gain[:, p * PIECE : (p + 1) * PIECE]).astype(BF16),
                    (values_b * gain[:, half + p * PIECE : half + (p + 1) * PIECE]).astype(BF16),
                ],
                axis=1,
            )
            gate = jnp.dot(scaled, w_gate[p], preferred_element_type=F32)
            up = jnp.dot(scaled, w_up[p], preferred_element_type=F32)
            if p == 0:
                squares[...] = square
                gate_sum[...] = gate
                up_sum[...] = up
            else:
                squares[...] += square
                gate_sum[...] += gate
                up_sum[...] += up
        mean = jnp.sum(squares[...], axis=-1, keepdims=True) * (1.0 / (2 * half))
        scale = lax.rsqrt(mean + 1e-05)
        gate = gate_sum[...] * scale
        hidden[...] = (gate / (1.0 + jnp.exp(-gate)) * (up_sum[...] * scale)).astype(BF16)

    def down(i):
        slot = lax.rem(i, 2)
        parity = lax.rem(i, 2)

        @pl.when(i >= 2)
        def _():
            sent_line(slot)

        def one(p, carry):
            share = jnp.dot(
                hidden[...], w_down[:, pl.ds(pl.multiple_of(p * PIECE, PIECE), PIECE)], preferred_element_type=F32
            )
            for k in range(SIDE):
                send_a[slot, p, k] = share[k * CHUNK : (k + 1) * CHUNK].astype(BF16)
            for step in range(1, SIDE):
                to = turn(x, step)
                remote(send_a.at[slot, p, to], part_a.at[i, p, step - 1], send1_sem.at[0, slot], recv_sem.at[0, i, p], on(stage, to, y)).start()
            share = jnp.dot(
                hidden[...], w_down[:, pl.ds(pl.multiple_of(half + p * PIECE, PIECE), PIECE)], preferred_element_type=F32
            )
            for j in range(SIDE // 2):
                groups = [share[m * CHUNK + j * OWN : m * CHUNK + (j + 1) * OWN] for m in range(SIDE)]
                send_b[slot, p, 2 * j + parity] = jnp.concatenate(groups[0::2], axis=0).astype(BF16)
                send_b[slot, p, 2 * j + 1 - parity] = jnp.concatenate(groups[1::2], axis=0).astype(BF16)
            for step in range(1, SIDE):
                to = turn(y, step)
                remote(send_b.at[slot, p, to], part_b.at[i, p, step - 1], send1_sem.at[1, slot], recv_sem.at[1, i, p], on(stage, x, to)).start()
            return carry

        lax.fori_loop(0, pieces, one, 0)

    def sent_line(slot):
        wait_bytes(send_a.at[slot, :, pl.ds(0, SIDE - 1)], send1_sem.at[0, slot])
        wait_bytes(send_b.at[slot, :, pl.ds(0, SIDE - 1)], send1_sem.at[1, slot])

    def reduce_line(i):
        slot = lax.rem(i, 2)

        def add(p, send, mine, part, total, entry):
            value = send[slot, p, mine].astype(F32)
            for k in range(SIDE - 1):
                value += part[i, p, k].astype(F32)
            total[i, p, entry] = value.astype(BF16)

        def one(p, carry):
            wait_bytes(part_a.at[i, p], recv_sem.at[0, i, p])
            add(p, send_a, x, part_a, sum_a, y)
            for step in range(1, SIDE):
                remote(sum_a.at[i, p, y], sum_a.at[i, p, y], send_sem.at[0, i], recv_sem.at[2, i, p], on(stage, x, turn(y, step))).start()
            wait_bytes(part_b.at[i, p], recv_sem.at[1, i, p])
            add(p, send_b, y, part_b, sum_b, x)
            for step in range(1, SIDE):
                remote(sum_b.at[i, p, x], sum_b.at[i, p, x], send_sem.at[1, i], recv_sem.at[3, i, p], on(stage, turn(x, step), y)).start()
            return carry

        lax.fori_loop(0, pieces, one, 0)

    def finish(i):
        def add(p, act, mine, total, out, own_at, column):
            branch = total[i, p, 0].astype(F32)
            for k in range(1, SIDE):
                branch += total[i, p, k].astype(F32)
            value = act[i, p, mine].astype(F32) + branch
            out[i, p] = value.astype(BF16)

            @pl.when(lax.rem(x + y + i, 2) == 0)
            def _():
                fresh[...] = value
                own = fresh[pl.ds(pl.multiple_of(own_at // 2 * OWN, OWN), OWN), :]
                states[i // 2, :, pl.ds(pl.multiple_of(column + p * PIECE, PIECE), PIECE)] = own.astype(BF16)

        def one(p, carry):
            wait_bytes(sum_a.at[i, p, pl.ds(0, SIDE - 1)], recv_sem.at[2, i, p])
            add(p, act_a, x, sum_a, out_a, y, 0)

            @pl.when(stage < stages - 1)
            def _():
                spread_a(i, p, stage + 1)

            wait_bytes(sum_b.at[i, p, pl.ds(0, SIDE - 1)], recv_sem.at[3, i, p])
            add(p, act_b, y, sum_b, out_b, x, half)

            @pl.when(stage < stages - 1)
            def _():
                spread_b(i, p, stage + 1)

            return carry

        lax.fori_loop(0, pieces, one, 0)

    work = {"up": up, "down": down, "line": reduce_line, "finish": finish}

    def advance(step, carry):
        for name, lag in ORDER:
            i = step - lag

            @pl.when((i >= 0) & (i < blocks))
            def _(name=name, i=i):
                work[name](i)

        return carry

    lags = [lag for _, lag in ORDER]
    lax.fori_loop(min(lags), blocks + max(lags), advance, 0)

    def drain(i, carry):
        wait_bytes(sum_a.at[i, :, pl.ds(0, SIDE - 1)], send_sem.at[0, i])
        wait_bytes(sum_b.at[i, :, pl.ds(0, SIDE - 1)], send_sem.at[1, i])

        @pl.when(stage < stages - 1)
        def _():
            spread_sent(i)

        return carry

    lax.fori_loop(0, blocks, drain, 0)
    for slot in range(2):
        sent_line(slot)


def solution(mesh):
    stages = mesh.shape["pipe"]

    def local(tokens, norm_gain, gate_weight, up_weight, down_weight):
        blocks, _, width = tokens.shape
        blocks *= 2
        units = gate_weight.shape[2]
        half = width // 2
        pieces = half // PIECE
        vmem = pl.BlockSpec(memory_space=pltpu.VMEM)
        hbm = pl.BlockSpec(memory_space=pl.ANY)
        dma = pltpu.SemaphoreType.DMA
        states = pl.pallas_call(
            functools.partial(kernel, stages, blocks),
            out_shape=jax.ShapeDtypeStruct(tokens.shape, BF16),
            in_specs=[vmem, vmem, hbm, hbm, hbm],
            out_specs=vmem,
            scratch_shapes=[
                pltpu.VMEM((pieces, 2 * PIECE, units), BF16),
                pltpu.VMEM((pieces, 2 * PIECE, units), BF16),
                pltpu.VMEM((units, width), BF16),
                pltpu.VMEM((blocks, pieces, SIDE, CHUNK, PIECE), BF16),
                pltpu.VMEM((blocks, pieces, SIDE, CHUNK, PIECE), BF16),
                pltpu.VMEM((blocks, pieces, SIDE - 1, CHUNK, PIECE), BF16),
                pltpu.VMEM((blocks, pieces, SIDE - 1, CHUNK, PIECE), BF16),
                pltpu.VMEM((blocks, pieces, SIDE, CHUNK, PIECE), BF16),
                pltpu.VMEM((blocks, pieces, SIDE, CHUNK, PIECE), BF16),
                pltpu.VMEM((2, pieces, SIDE, CHUNK, PIECE), BF16),
                pltpu.VMEM((2, pieces, SIDE, CHUNK, PIECE), BF16),
                pltpu.VMEM((blocks, pieces, CHUNK, PIECE), BF16),
                pltpu.VMEM((blocks, pieces, CHUNK, PIECE), BF16),
                pltpu.VMEM((blocks // 4, SIDE, 2 * OWN, half), BF16),
                pltpu.VMEM((blocks // 4, SIDE, 2 * OWN, half), BF16),
                pltpu.VMEM((SIDE * CHUNK, units), F32),
                pltpu.VMEM((SIDE * CHUNK, units), F32),
                pltpu.VMEM((SIDE * CHUNK, 128), F32),
                pltpu.VMEM((SIDE * CHUNK, units), BF16),
                pltpu.VMEM((CHUNK, PIECE), F32),
                dma((4 * pieces + 1,)),
                dma((6, blocks, pieces)),
                dma((2, 2)),
                dma((4, blocks)),
                dma((4, blocks // 4)),
            ],
            compiler_params=pltpu.CompilerParams(
                collective_id=0, has_side_effects=True, vmem_limit_bytes=62 * 2**20
            ),
            cost_estimate=pl.CostEstimate(
                flops=2 * 3 * blocks * SIDE * CHUNK * width * units,
                bytes_accessed=6 * width * units,
                transcendentals=blocks * SIDE * CHUNK * units,
            ),
        )(tokens, norm_gain, gate_weight[0], up_weight[0], down_weight[0])
        return states[None]

    in_specs = (
        P(None, "tensor", None),
        P("pipe", None),
        P("pipe", None, "tensor"),
        P("pipe", None, "tensor"),
        P("pipe", "tensor", None),
    )
    out_specs = P("pipe", None, "tensor", None)
    return jax.shard_map(local, mesh=mesh, in_specs=in_specs, out_specs=out_specs, check_vma=False)
```

```python
import functools

import jax
import jax.numpy as jnp
from jax import lax
from jax.experimental import pallas as pl
from jax.experimental.pallas import tpu as pltpu
from jax.sharding import PartitionSpec as P

MESH = pl.DeviceIdType.MESH
F32 = jnp.float32
BF16 = jnp.bfloat16

SIDE = 4
OWN = 8
CHUNK = SIDE // 2 * OWN
PIECE = 512
ORDER = (
    ("down", 0, 0, 2),
    ("finish", 1, 0, 1),
    ("down", 0, 2, 4),
    ("finish", 1, 1, 3),
    ("up", -1, 0, 2),
    ("line", 0, 0, 1),
    ("finish", 1, 3, 4),
    ("line", 0, 1, 2),
    ("up", -1, 2, 3),
    ("line", 0, 2, 4),
    ("up", -1, 3, 4),
)


def kernel(
    stages, blocks, tokens, gain, w_gate_hbm, w_up_hbm, w_down_hbm, states,
    w_gate, w_up, w_down, act_a, act_b, part_a, part_b, sum_a, sum_b, send_a, send_b,
    out_a, out_b, tok_a, tok_b, gate_sum, up_sum, squares, hidden, fresh, load_sem, recv_sem, send1_sem, send_sem, tok_sem,
):
    stage = lax.axis_index("pipe")
    place = lax.axis_index("tensor")
    x, y = place // SIDE, lax.rem(place, SIDE)
    pieces = act_a.shape[1]
    half = pieces * PIECE
    pairs = blocks // 4

    def on(stage_to, x_to, y_to):
        return (stage_to, x_to * SIDE + y_to)

    def turn(value, step):
        return lax.rem(value + step, SIDE)

    loads = []
    for p in range(pieces):
        for k in range(2):
            for j, (source, target) in enumerate(((w_gate_hbm, w_gate), (w_up_hbm, w_up))):
                loads.append(
                    pltpu.make_async_copy(
                        source.at[pl.ds(k * half + p * PIECE, PIECE)],
                        target.at[p, pl.ds(k * PIECE, PIECE)],
                        load_sem.at[(p * 2 + k) * 2 + j],
                    )
                )
    loads.append(pltpu.make_async_copy(w_down_hbm, w_down, load_sem.at[4 * pieces]))
    for load in loads:
        load.start()

    barrier = pltpu.get_barrier_semaphore()
    after, before = lax.rem(stage + 1, stages), lax.rem(stage + stages - 1, stages)
    source = jnp.where(stage == 0, after, before)
    for other in (stage, source):
        for step in range(1, SIDE):
            for target in (on(other, turn(x, step), y), on(other, x, turn(y, step))):
                pl.semaphore_signal(barrier, inc=1, device_id=target, device_id_type=MESH)
    pl.semaphore_signal(barrier, inc=1, device_id=on(source, x, y), device_id_type=MESH)
    line = 2 * (SIDE - 1)
    greeted = line + jnp.where(stage == stages - 1, 0, line + 1) + jnp.where(stage == 1, line + 1, 0)
    pl.semaphore_wait(barrier, greeted)

    def remote(source, target, sent, received, device):
        return pltpu.make_async_remote_copy(
            src_ref=source, dst_ref=target, send_sem=sent, recv_sem=received, device_id=device, device_id_type=MESH
        )

    def wait_bytes(ref, sem):
        pltpu.make_async_copy(ref, ref, sem).wait()

    def spread_a(i, p, stage_to):
        for step in range(SIDE):
            remote(out_a.at[i, p], act_a.at[i, p, x], send_sem.at[2, i], recv_sem.at[4, i, p], on(stage_to, turn(x, step), y)).start()

    def spread_b(i, p, stage_to):
        for step in range(SIDE):
            remote(out_b.at[i, p], act_b.at[i, p, y], send_sem.at[3, i], recv_sem.at[5, i, p], on(stage_to, x, turn(y, step))).start()

    def spread_sent(i):
        wait_bytes(act_a.at[i], send_sem.at[2, i])
        wait_bytes(act_b.at[i], send_sem.at[3, i])

    @pl.when(stage == 1)
    def _():
        for pair in range(pairs):
            rows = jnp.concatenate([tokens[2 * pair].astype(F32), tokens[2 * pair + 1].astype(F32)], axis=0).astype(BF16)
            tok_a[pair, y] = rows[:, :half]
            tok_b[pair, x] = rows[:, half:]
            for step in range(1, SIDE):
                remote(tok_a.at[pair, y], tok_a.at[pair, y], tok_sem.at[0, pair], tok_sem.at[2, pair], on(stage, x, turn(y, step))).start()
                remote(tok_b.at[pair, x], tok_b.at[pair, x], tok_sem.at[1, pair], tok_sem.at[3, pair], on(stage, turn(x, step), y)).start()

        def bring(pair, carry):
            wait_bytes(tok_a.at[pair, pl.ds(0, SIDE - 1)], tok_sem.at[2, pair])
            wait_bytes(tok_b.at[pair, pl.ds(0, SIDE - 1)], tok_sem.at[3, pair])
            for half_of_pair in range(2):
                for parity in range(2):
                    i = 4 * pair + 2 * half_of_pair + parity
                    for p in range(pieces):
                        at = slice(p * PIECE, (p + 1) * PIECE)
                        own = slice(half_of_pair * OWN, (half_of_pair + 1) * OWN)
                        for tok, out, mine in ((tok_a, out_a, x), (tok_b, out_b, y)):
                            first = lax.rem(mine + parity, 2)
                            out[i, p] = jnp.concatenate(
                                [tok[pair, first + 2 * k, :, at].astype(F32)[own] for k in range(SIDE // 2)], axis=0
                            ).astype(BF16)
                        spread_a(i, p, stage - 1)
                        spread_b(i, p, stage - 1)
            return carry

        lax.fori_loop(0, pairs, bring, 0)

        def brought(pair, carry):
            wait_bytes(tok_a.at[pair, pl.ds(0, SIDE - 1)], tok_sem.at[0, pair])
            wait_bytes(tok_b.at[pair, pl.ds(0, SIDE - 1)], tok_sem.at[1, pair])
            for k in range(4):
                spread_sent(4 * pair + k)
            return carry

        lax.fori_loop(0, pairs, brought, 0)

    for load in loads:
        load.wait()

    def up(i, first, last):
        rows = SIDE * CHUNK
        parity = lax.rem(i, 2)

        for p in range(first, last):
            wait_bytes(act_a.at[i, p], recv_sem.at[4, i, p])
            wait_bytes(act_b.at[i, p], recv_sem.at[5, i, p])
            values_a = act_a[i, p].astype(F32).reshape(rows, PIECE)
            even = [act_b[i, p, 2 * j + parity].astype(F32) for j in range(SIDE // 2)]
            odd = [act_b[i, p, 2 * j + 1 - parity].astype(F32) for j in range(SIDE // 2)]
            values_b = jnp.concatenate(
                [
                    (odd if m % 2 else even)[j][m // 2 * OWN : (m // 2 + 1) * OWN]
                    for m in range(SIDE)
                    for j in range(SIDE // 2)
                ],
                axis=0,
            )
            square = jnp.zeros((rows, 128), F32)
            for values in (values_a, values_b):
                for lane in range(0, PIECE, 128):
                    part = values[:, lane : lane + 128]
                    square += part * part
            scaled = jnp.concatenate(
                [
                    (values_a * gain[:, p * PIECE : (p + 1) * PIECE]).astype(BF16),
                    (values_b * gain[:, half + p * PIECE : half + (p + 1) * PIECE]).astype(BF16),
                ],
                axis=1,
            )
            gate = jnp.dot(scaled, w_gate[p], preferred_element_type=F32)
            up = jnp.dot(scaled, w_up[p], preferred_element_type=F32)
            if p == 0:
                squares[...] = square
                gate_sum[...] = gate
                up_sum[...] = up
            else:
                squares[...] += square
                gate_sum[...] += gate
                up_sum[...] += up
        if last == pieces:
            mean = jnp.sum(squares[...], axis=-1, keepdims=True) * (1.0 / (2 * half))
            scale = lax.rsqrt(mean + 1e-05)
            gate = gate_sum[...] * scale
            hidden[...] = (gate / (1.0 + jnp.exp(-gate)) * (up_sum[...] * scale)).astype(BF16)

    def down(i, first, last):
        slot = lax.rem(i, 2)
        parity = lax.rem(i, 2)

        if first == 0:

            @pl.when(i >= 2)
            def _():
                sent_line(slot)

        def one(p, carry):
            share = jnp.dot(
                hidden[...], w_down[:, pl.ds(pl.multiple_of(p * PIECE, PIECE), PIECE)], preferred_element_type=F32
            )
            for k in range(SIDE):
                send_a[slot, p, k] = share[k * CHUNK : (k + 1) * CHUNK].astype(BF16)
            for step in range(1, SIDE):
                to = turn(x, step)
                remote(send_a.at[slot, p, to], part_a.at[i, p, step - 1], send1_sem.at[0, slot], recv_sem.at[0, i, p], on(stage, to, y)).start()
            share = jnp.dot(
                hidden[...], w_down[:, pl.ds(pl.multiple_of(half + p * PIECE, PIECE), PIECE)], preferred_element_type=F32
            )
            for j in range(SIDE // 2):
                groups = [share[m * CHUNK + j * OWN : m * CHUNK + (j + 1) * OWN] for m in range(SIDE)]
                send_b[slot, p, 2 * j + parity] = jnp.concatenate(groups[0::2], axis=0).astype(BF16)
                send_b[slot, p, 2 * j + 1 - parity] = jnp.concatenate(groups[1::2], axis=0).astype(BF16)
            for step in range(1, SIDE):
                to = turn(y, step)
                remote(send_b.at[slot, p, to], part_b.at[i, p, step - 1], send1_sem.at[1, slot], recv_sem.at[1, i, p], on(stage, x, to)).start()
            return carry

        lax.fori_loop(first, last, one, 0)

    def sent_line(slot):
        wait_bytes(send_a.at[slot, :, pl.ds(0, SIDE - 1)], send1_sem.at[0, slot])
        wait_bytes(send_b.at[slot, :, pl.ds(0, SIDE - 1)], send1_sem.at[1, slot])

    def reduce_line(i, first, last):
        slot = lax.rem(i, 2)

        def add(p, send, mine, part, total, entry):
            value = send[slot, p, mine].astype(F32)
            for k in range(SIDE - 1):
                value += part[i, p, k].astype(F32)
            total[i, p, entry] = value.astype(BF16)

        def one(p, carry):
            wait_bytes(part_a.at[i, p], recv_sem.at[0, i, p])
            add(p, send_a, x, part_a, sum_a, y)
            for step in range(1, SIDE):
                remote(sum_a.at[i, p, y], sum_a.at[i, p, y], send_sem.at[0, i], recv_sem.at[2, i, p], on(stage, x, turn(y, step))).start()
            wait_bytes(part_b.at[i, p], recv_sem.at[1, i, p])
            add(p, send_b, y, part_b, sum_b, x)
            for step in range(1, SIDE):
                remote(sum_b.at[i, p, x], sum_b.at[i, p, x], send_sem.at[1, i], recv_sem.at[3, i, p], on(stage, turn(x, step), y)).start()
            return carry

        lax.fori_loop(first, last, one, 0)

    def finish(i, first, last):
        def add(p, act, mine, total, out, own_at, column):
            branch = total[i, p, 0].astype(F32)
            for k in range(1, SIDE):
                branch += total[i, p, k].astype(F32)
            value = act[i, p, mine].astype(F32) + branch
            out[i, p] = value.astype(BF16)

            @pl.when(lax.rem(x + y + i, 2) == 0)
            def _():
                fresh[...] = value
                own = fresh[pl.ds(pl.multiple_of(own_at // 2 * OWN, OWN), OWN), :]
                states[i // 2, :, pl.ds(pl.multiple_of(column + p * PIECE, PIECE), PIECE)] = own.astype(BF16)

        def one(p, carry):
            wait_bytes(sum_a.at[i, p, pl.ds(0, SIDE - 1)], recv_sem.at[2, i, p])
            add(p, act_a, x, sum_a, out_a, y, 0)

            @pl.when(stage < stages - 1)
            def _():
                spread_a(i, p, stage + 1)

            wait_bytes(sum_b.at[i, p, pl.ds(0, SIDE - 1)], recv_sem.at[3, i, p])
            add(p, act_b, y, sum_b, out_b, x, half)

            @pl.when(stage < stages - 1)
            def _():
                spread_b(i, p, stage + 1)

            return carry

        lax.fori_loop(first, last, one, 0)

    work = {"up": up, "down": down, "line": reduce_line, "finish": finish}

    def advance(step, carry):
        for name, lag, first, last in ORDER:
            i = step - lag

            @pl.when((i >= 0) & (i < blocks))
            def _(name=name, i=i, first=first, last=last):
                work[name](i, first, last)

        return carry

    lags = [entry[1] for entry in ORDER]
    lax.fori_loop(min(lags), blocks + max(lags), advance, 0)

    def drain(i, carry):
        wait_bytes(sum_a.at[i, :, pl.ds(0, SIDE - 1)], send_sem.at[0, i])
        wait_bytes(sum_b.at[i, :, pl.ds(0, SIDE - 1)], send_sem.at[1, i])

        @pl.when(stage < stages - 1)
        def _():
            spread_sent(i)

        return carry

    lax.fori_loop(0, blocks, drain, 0)
    for slot in range(2):
        sent_line(slot)


def solution(mesh):
    stages = mesh.shape["pipe"]

    def local(tokens, norm_gain, gate_weight, up_weight, down_weight):
        blocks, _, width = tokens.shape
        blocks *= 2
        units = gate_weight.shape[2]
        half = width // 2
        pieces = half // PIECE
        vmem = pl.BlockSpec(memory_space=pltpu.VMEM)
        hbm = pl.BlockSpec(memory_space=pl.ANY)
        dma = pltpu.SemaphoreType.DMA
        states = pl.pallas_call(
            functools.partial(kernel, stages, blocks),
            out_shape=jax.ShapeDtypeStruct(tokens.shape, BF16),
            in_specs=[vmem, vmem, hbm, hbm, hbm],
            out_specs=vmem,
            scratch_shapes=[
                pltpu.VMEM((pieces, 2 * PIECE, units), BF16),
                pltpu.VMEM((pieces, 2 * PIECE, units), BF16),
                pltpu.VMEM((units, width), BF16),
                pltpu.VMEM((blocks, pieces, SIDE, CHUNK, PIECE), BF16),
                pltpu.VMEM((blocks, pieces, SIDE, CHUNK, PIECE), BF16),
                pltpu.VMEM((blocks, pieces, SIDE - 1, CHUNK, PIECE), BF16),
                pltpu.VMEM((blocks, pieces, SIDE - 1, CHUNK, PIECE), BF16),
                pltpu.VMEM((blocks, pieces, SIDE, CHUNK, PIECE), BF16),
                pltpu.VMEM((blocks, pieces, SIDE, CHUNK, PIECE), BF16),
                pltpu.VMEM((2, pieces, SIDE, CHUNK, PIECE), BF16),
                pltpu.VMEM((2, pieces, SIDE, CHUNK, PIECE), BF16),
                pltpu.VMEM((blocks, pieces, CHUNK, PIECE), BF16),
                pltpu.VMEM((blocks, pieces, CHUNK, PIECE), BF16),
                pltpu.VMEM((blocks // 4, SIDE, 2 * OWN, half), BF16),
                pltpu.VMEM((blocks // 4, SIDE, 2 * OWN, half), BF16),
                pltpu.VMEM((SIDE * CHUNK, units), F32),
                pltpu.VMEM((SIDE * CHUNK, units), F32),
                pltpu.VMEM((SIDE * CHUNK, 128), F32),
                pltpu.VMEM((SIDE * CHUNK, units), BF16),
                pltpu.VMEM((CHUNK, PIECE), F32),
                dma((4 * pieces + 1,)),
                dma((6, blocks, pieces)),
                dma((2, 2)),
                dma((4, blocks)),
                dma((4, blocks // 4)),
            ],
            compiler_params=pltpu.CompilerParams(
                collective_id=0, has_side_effects=True, vmem_limit_bytes=62 * 2**20
            ),
            cost_estimate=pl.CostEstimate(
                flops=2 * 3 * blocks * SIDE * CHUNK * width * units,
                bytes_accessed=6 * width * units,
                transcendentals=blocks * SIDE * CHUNK * units,
            ),
        )(tokens, norm_gain, gate_weight[0], up_weight[0], down_weight[0])
        return states[None]

    in_specs = (
        P(None, "tensor", None),
        P("pipe", None),
        P("pipe", None, "tensor"),
        P("pipe", None, "tensor"),
        P("pipe", "tensor", None),
    )
    out_specs = P("pipe", None, "tensor", None)
    return jax.shard_map(local, mesh=mesh, in_specs=in_specs, out_specs=out_specs, check_vma=False)
```

```python
import functools

import jax
import jax.numpy as jnp
from jax import lax
from jax.experimental import pallas as pl
from jax.experimental.pallas import tpu as pltpu
from jax.sharding import PartitionSpec as P

MESH = pl.DeviceIdType.MESH
F32 = jnp.float32
BF16 = jnp.bfloat16

SIDE = 4
OWN = 8
CHUNK = SIDE // 2 * OWN
PIECE = 512
ORDER = (
    ("down", 0, 0, 2),
    ("finish", 1, 0, 1),
    ("down", 0, 2, 4),
    ("finish", 1, 1, 3),
    ("up", -1, 0, 2),
    ("line", 0, 0, 1),
    ("finish", 1, 3, 4),
    ("line", 0, 1, 2),
    ("up", -1, 2, 3),
    ("line", 0, 2, 4),
    ("up", -1, 3, 4),
)
NEAR = 6


def kernel(
    stages, blocks, tokens, gain, w_gate_hbm, w_up_hbm, w_down_hbm, states,
    w_gate, w_up, w_down, act_a, act_b, part_a, part_b, sum_a, sum_b, send_a, send_b,
    out_a, out_b, tok_a, tok_b, gate_sum, up_sum, squares, hidden, fresh, load_sem, recv_sem, send1_sem, send_sem, tok_sem,
):
    stage = lax.axis_index("pipe")
    place = lax.axis_index("tensor")
    x, y = place // SIDE, lax.rem(place, SIDE)
    pieces = act_a.shape[1]
    half = pieces * PIECE
    pairs = blocks // 4

    def on(stage_to, x_to, y_to):
        return (stage_to, x_to * SIDE + y_to)

    def turn(value, step):
        return lax.rem(value + step, SIDE)

    loads = []
    for p in range(pieces):
        for k in range(2):
            for j, (source, target) in enumerate(((w_gate_hbm, w_gate), (w_up_hbm, w_up))):
                loads.append(
                    pltpu.make_async_copy(
                        source.at[pl.ds(k * half + p * PIECE, PIECE)],
                        target.at[p, pl.ds(k * PIECE, PIECE)],
                        load_sem.at[(p * 2 + k) * 2 + j],
                    )
                )
    loads.append(pltpu.make_async_copy(w_down_hbm, w_down, load_sem.at[4 * pieces]))
    for load in loads:
        load.start()

    barrier = pltpu.get_barrier_semaphore()
    after, before = lax.rem(stage + 1, stages), lax.rem(stage + stages - 1, stages)
    def greet(other, steps):
        for step in steps:
            for target in (on(other, turn(x, step), y), on(other, x, turn(y, step))) if step else (on(other, x, y),):
                pl.semaphore_signal(barrier, inc=1, device_id=target, device_id_type=MESH)

    greet(before, range(SIDE))
    greet(stage, range(1, SIDE))

    @pl.when(stage == 0)
    def _():
        greet(after, range(SIDE))

    line = 2 * (SIDE - 1)
    greeted = 2 * line + 1 + jnp.where(stage == 1, line + 1, 0)
    pl.semaphore_wait(barrier, greeted)

    def remote(source, target, sent, received, device):
        return pltpu.make_async_remote_copy(
            src_ref=source, dst_ref=target, send_sem=sent, recv_sem=received, device_id=device, device_id_type=MESH
        )

    def wait_bytes(ref, sem):
        pltpu.make_async_copy(ref, ref, sem).wait()

    def spread_a(i, p, stage_to):
        for step in range(SIDE):
            remote(out_a.at[i, p], act_a.at[i, p, x], send_sem.at[2, i], recv_sem.at[4, i, p], on(stage_to, turn(x, step), y)).start()

    def spread_b(i, p, stage_to):
        for step in range(SIDE):
            remote(out_b.at[i, p], act_b.at[i, p, y], send_sem.at[3, i], recv_sem.at[5, i, p], on(stage_to, x, turn(y, step))).start()

    def spread_sent(i):
        wait_bytes(act_a.at[i], send_sem.at[2, i])
        wait_bytes(act_b.at[i], send_sem.at[3, i])

    @pl.when((stage == 1) | (stage == stages - 1))
    def _():
        for pair in range(pairs):
            rows = jnp.concatenate([tokens[2 * pair].astype(F32), tokens[2 * pair + 1].astype(F32)], axis=0).astype(BF16)
            tok_a[pair, y] = rows[:, :half]
            tok_b[pair, x] = rows[:, half:]
            for step in range(1, SIDE):
                remote(tok_a.at[pair, y], tok_a.at[pair, y], tok_sem.at[0, pair], tok_sem.at[2, pair], on(stage, x, turn(y, step))).start()
                remote(tok_b.at[pair, x], tok_b.at[pair, x], tok_sem.at[1, pair], tok_sem.at[3, pair], on(stage, turn(x, step), y)).start()

        def arrived(pair, carry):
            wait_bytes(tok_a.at[pair, pl.ds(0, SIDE - 1)], tok_sem.at[2, pair])
            wait_bytes(tok_b.at[pair, pl.ds(0, SIDE - 1)], tok_sem.at[3, pair])
            return carry

        def bring(i, carry):
            pair, second, parity = i // 4, lax.rem(i // 2, 2), lax.rem(i, 2)
            for p in range(pieces):
                at = slice(p * PIECE, (p + 1) * PIECE)
                for tok, out, mine in ((tok_a, out_a, x), (tok_b, out_b, y)):
                    rows = [tok[pair, lax.rem(mine + parity, 2) + 2 * k, :, at].astype(F32) for k in range(SIDE // 2)]
                    rows = [jnp.where(second == 0, value[:OWN], value[OWN:]) for value in rows]
                    out[i, p] = jnp.concatenate(rows, axis=0).astype(BF16)
                spread_a(i, p, 0)
                spread_b(i, p, 0)
            return carry

        def brought(pair, carry):
            wait_bytes(tok_a.at[pair, pl.ds(0, SIDE - 1)], tok_sem.at[0, pair])
            wait_bytes(tok_b.at[pair, pl.ds(0, SIDE - 1)], tok_sem.at[1, pair])
            return carry

        def sent(i, carry):
            spread_sent(i)
            return carry

        first = jnp.where(stage == 1, 0, NEAR)
        last = jnp.where(stage == 1, NEAR, blocks)
        arrived(0, 0)

        @pl.when(stage == 1)
        def _():
            lax.fori_loop(0, min(4, NEAR), bring, 0)

        lax.fori_loop(1, pairs, arrived, 0)
        lax.fori_loop(jnp.where(stage == 1, min(4, NEAR), NEAR), last, bring, 0)

        lax.fori_loop(0, pairs, brought, 0)
        lax.fori_loop(first, last, sent, 0)

    for load in loads:
        load.wait()

    def up(i, first, last):
        rows = SIDE * CHUNK
        parity = lax.rem(i, 2)

        for p in range(first, last):
            wait_bytes(act_a.at[i, p], recv_sem.at[4, i, p])
            wait_bytes(act_b.at[i, p], recv_sem.at[5, i, p])
            values_a = act_a[i, p].astype(F32).reshape(rows, PIECE)
            even = [act_b[i, p, 2 * j + parity].astype(F32) for j in range(SIDE // 2)]
            odd = [act_b[i, p, 2 * j + 1 - parity].astype(F32) for j in range(SIDE // 2)]
            values_b = jnp.concatenate(
                [
                    (odd if m % 2 else even)[j][m // 2 * OWN : (m // 2 + 1) * OWN]
                    for m in range(SIDE)
                    for j in range(SIDE // 2)
                ],
                axis=0,
            )
            square = jnp.zeros((rows, 128), F32)
            for values in (values_a, values_b):
                for lane in range(0, PIECE, 128):
                    part = values[:, lane : lane + 128]
                    square += part * part
            scaled = jnp.concatenate(
                [
                    (values_a * gain[:, p * PIECE : (p + 1) * PIECE]).astype(BF16),
                    (values_b * gain[:, half + p * PIECE : half + (p + 1) * PIECE]).astype(BF16),
                ],
                axis=1,
            )
            gate = jnp.dot(scaled, w_gate[p], preferred_element_type=F32)
            up = jnp.dot(scaled, w_up[p], preferred_element_type=F32)
            if p == 0:
                squares[...] = square
                gate_sum[...] = gate
                up_sum[...] = up
            else:
                squares[...] += square
                gate_sum[...] += gate
                up_sum[...] += up
        if last == pieces:
            mean = jnp.sum(squares[...], axis=-1, keepdims=True) * (1.0 / (2 * half))
            scale = lax.rsqrt(mean + 1e-05)
            gate = gate_sum[...] * scale
            hidden[...] = (gate / (1.0 + jnp.exp(-gate)) * (up_sum[...] * scale)).astype(BF16)

    def down(i, first, last):
        slot = lax.rem(i, 2)
        parity = lax.rem(i, 2)

        if first == 0:

            @pl.when(i >= 2)
            def _():
                sent_line(slot)

        def one(p, carry):
            share = jnp.dot(
                hidden[...], w_down[:, pl.ds(pl.multiple_of(p * PIECE, PIECE), PIECE)], preferred_element_type=F32
            )
            for k in range(SIDE):
                send_a[slot, p, k] = share[k * CHUNK : (k + 1) * CHUNK].astype(BF16)
            for step in range(1, SIDE):
                to = turn(x, step)
                remote(send_a.at[slot, p, to], part_a.at[i, p, step - 1], send1_sem.at[0, slot], recv_sem.at[0, i, p], on(stage, to, y)).start()
            share = jnp.dot(
                hidden[...], w_down[:, pl.ds(pl.multiple_of(half + p * PIECE, PIECE), PIECE)], preferred_element_type=F32
            )
            for j in range(SIDE // 2):
                groups = [share[m * CHUNK + j * OWN : m * CHUNK + (j + 1) * OWN] for m in range(SIDE)]
                send_b[slot, p, 2 * j + parity] = jnp.concatenate(groups[0::2], axis=0).astype(BF16)
                send_b[slot, p, 2 * j + 1 - parity] = jnp.concatenate(groups[1::2], axis=0).astype(BF16)
            for step in range(1, SIDE):
                to = turn(y, step)
                remote(send_b.at[slot, p, to], part_b.at[i, p, step - 1], send1_sem.at[1, slot], recv_sem.at[1, i, p], on(stage, x, to)).start()
            return carry

        lax.fori_loop(first, last, one, 0)

    def sent_line(slot):
        wait_bytes(send_a.at[slot, :, pl.ds(0, SIDE - 1)], send1_sem.at[0, slot])
        wait_bytes(send_b.at[slot, :, pl.ds(0, SIDE - 1)], send1_sem.at[1, slot])

    def reduce_line(i, first, last):
        slot = lax.rem(i, 2)

        def add(p, send, mine, part, total, entry):
            value = send[slot, p, mine].astype(F32)
            for k in range(SIDE - 1):
                value += part[i, p, k].astype(F32)
            total[i, p, entry] = value.astype(BF16)

        def one(p, carry):
            wait_bytes(part_a.at[i, p], recv_sem.at[0, i, p])
            add(p, send_a, x, part_a, sum_a, y)
            for step in range(1, SIDE):
                remote(sum_a.at[i, p, y], sum_a.at[i, p, y], send_sem.at[0, i], recv_sem.at[2, i, p], on(stage, x, turn(y, step))).start()
            wait_bytes(part_b.at[i, p], recv_sem.at[1, i, p])
            add(p, send_b, y, part_b, sum_b, x)
            for step in range(1, SIDE):
                remote(sum_b.at[i, p, x], sum_b.at[i, p, x], send_sem.at[1, i], recv_sem.at[3, i, p], on(stage, turn(x, step), y)).start()
            return carry

        lax.fori_loop(first, last, one, 0)

    def finish(i, first, last):
        def add(p, act, mine, total, out, own_at, column):
            branch = total[i, p, 0].astype(F32)
            for k in range(1, SIDE):
                branch += total[i, p, k].astype(F32)
            value = act[i, p, mine].astype(F32) + branch
            out[i, p] = value.astype(BF16)

            @pl.when(lax.rem(x + y + i, 2) == 0)
            def _():
                fresh[...] = value
                own = fresh[pl.ds(pl.multiple_of(own_at // 2 * OWN, OWN), OWN), :]
                states[i // 2, :, pl.ds(pl.multiple_of(column + p * PIECE, PIECE), PIECE)] = own.astype(BF16)

        def one(p, carry):
            wait_bytes(sum_a.at[i, p, pl.ds(0, SIDE - 1)], recv_sem.at[2, i, p])
            add(p, act_a, x, sum_a, out_a, y, 0)

            @pl.when(stage < stages - 1)
            def _():
                spread_a(i, p, stage + 1)

            wait_bytes(sum_b.at[i, p, pl.ds(0, SIDE - 1)], recv_sem.at[3, i, p])
            add(p, act_b, y, sum_b, out_b, x, half)

            @pl.when(stage < stages - 1)
            def _():
                spread_b(i, p, stage + 1)

            return carry

        lax.fori_loop(first, last, one, 0)

    work = {"up": up, "down": down, "line": reduce_line, "finish": finish}

    def advance(step, carry):
        for name, lag, first, last in ORDER:
            i = step - lag

            @pl.when((i >= 0) & (i < blocks))
            def _(name=name, i=i, first=first, last=last):
                work[name](i, first, last)

        return carry

    lags = [entry[1] for entry in ORDER]
    lax.fori_loop(min(lags), blocks + max(lags), advance, 0)

    def drain(i, carry):
        wait_bytes(sum_a.at[i, :, pl.ds(0, SIDE - 1)], send_sem.at[0, i])
        wait_bytes(sum_b.at[i, :, pl.ds(0, SIDE - 1)], send_sem.at[1, i])

        @pl.when(stage < stages - 1)
        def _():
            spread_sent(i)

        return carry

    lax.fori_loop(0, blocks, drain, 0)
    for slot in range(2):
        sent_line(slot)


def solution(mesh):
    stages = mesh.shape["pipe"]

    def local(tokens, norm_gain, gate_weight, up_weight, down_weight):
        blocks, _, width = tokens.shape
        blocks *= 2
        units = gate_weight.shape[2]
        half = width // 2
        pieces = half // PIECE
        vmem = pl.BlockSpec(memory_space=pltpu.VMEM)
        hbm = pl.BlockSpec(memory_space=pl.ANY)
        dma = pltpu.SemaphoreType.DMA
        states = pl.pallas_call(
            functools.partial(kernel, stages, blocks),
            out_shape=jax.ShapeDtypeStruct(tokens.shape, BF16),
            in_specs=[vmem, vmem, hbm, hbm, hbm],
            out_specs=vmem,
            scratch_shapes=[
                pltpu.VMEM((pieces, 2 * PIECE, units), BF16),
                pltpu.VMEM((pieces, 2 * PIECE, units), BF16),
                pltpu.VMEM((units, width), BF16),
                pltpu.VMEM((blocks, pieces, SIDE, CHUNK, PIECE), BF16),
                pltpu.VMEM((blocks, pieces, SIDE, CHUNK, PIECE), BF16),
                pltpu.VMEM((blocks, pieces, SIDE - 1, CHUNK, PIECE), BF16),
                pltpu.VMEM((blocks, pieces, SIDE - 1, CHUNK, PIECE), BF16),
                pltpu.VMEM((blocks, pieces, SIDE, CHUNK, PIECE), BF16),
                pltpu.VMEM((blocks, pieces, SIDE, CHUNK, PIECE), BF16),
                pltpu.VMEM((2, pieces, SIDE, CHUNK, PIECE), BF16),
                pltpu.VMEM((2, pieces, SIDE, CHUNK, PIECE), BF16),
                pltpu.VMEM((blocks, pieces, CHUNK, PIECE), BF16),
                pltpu.VMEM((blocks, pieces, CHUNK, PIECE), BF16),
                pltpu.VMEM((blocks // 4, SIDE, 2 * OWN, half), BF16),
                pltpu.VMEM((blocks // 4, SIDE, 2 * OWN, half), BF16),
                pltpu.VMEM((SIDE * CHUNK, units), F32),
                pltpu.VMEM((SIDE * CHUNK, units), F32),
                pltpu.VMEM((SIDE * CHUNK, 128), F32),
                pltpu.VMEM((SIDE * CHUNK, units), BF16),
                pltpu.VMEM((CHUNK, PIECE), F32),
                dma((4 * pieces + 1,)),
                dma((6, blocks, pieces)),
                dma((2, 2)),
                dma((4, blocks)),
                dma((4, blocks // 4)),
            ],
            compiler_params=pltpu.CompilerParams(
                collective_id=0, has_side_effects=True, vmem_limit_bytes=62 * 2**20
            ),
            cost_estimate=pl.CostEstimate(
                flops=2 * 3 * blocks * SIDE * CHUNK * width * units,
                bytes_accessed=6 * width * units,
                transcendentals=blocks * SIDE * CHUNK * units,
            ),
        )(tokens, norm_gain, gate_weight[0], up_weight[0], down_weight[0])
        return states[None]

    in_specs = (
        P(None, "tensor", None),
        P("pipe", None),
        P("pipe", None, "tensor"),
        P("pipe", None, "tensor"),
        P("pipe", "tensor", None),
    )
    out_specs = P("pipe", None, "tensor", None)
    return jax.shard_map(local, mesh=mesh, in_specs=in_specs, out_specs=out_specs, check_vma=False)
```
